128 devices in a mesh: tile: 32 (over y, x_lo, z), angle: 4 (over x_hi, core).
Axes of the slice: x: 4 (x_hi: 2, x_lo: 2; x = x_hi * 2 + x_lo), y: 4, z: 4, core: 2. Of those that a mesh axis runs over, the one named last changes fastest.
Arguments:
- volume: float32 [96, 1024, 256], P(None, 'tile'), may hold values from -6 to 6
- measured: float32 [2, 32, 512, 8192], P(None, 'angle', 'tile'), may hold values from -1536 to 1536
- blocks: float32 [2, 32, 96, 16, 96], P(None, 'angle', 'tile'), may hold values from 0.1 to 1
- ray_lists: int32 [2, 32, 96], P(None, 'angle', 'tile'), may hold values from 0 to 31, as said below
- counts: int32 [2, 32, 32], P(None, 'angle', 'tile'), may hold values from 1 to 3
Outputs:
- volume_final: float32 [96, 1024, 256], P(None, 'tile')
The draws below stay inside these ranges and needn't reach their ends.
Inputs may be any that keep to these rules, and one draw needn't show every extreme that they name: `ray_lists`: entry 3 * t + k names the ray tile that entry k of volume tile t touches: entry 0 is t itself, every entry lies within one ray tile of t. Only the first counts entries of a tile's list are used.
All inputs are finite; a program needn't handle non-finite values.
Results may differ from the reference program's by a relative error of at most 0.0001.
Values sent between devices are 32-bit elements; how exact they have to be, the bound alone decides.
A program may use at most 192 MiB of HBM per device.

```python
import jax
import jax.numpy as jnp
from jax import lax

NZ = 96
CY = 256
CX = 32
DR = 16
SLOTS = 3
SUBSETS = 2
NX = 1024
ANGLES = 32
RAYS = 512
CELLS = 8192
TILE_SLOTS = 96
N_TILE = 32


def draw_ray_lists(key, part):
    key = jax.random.fold_in(key, 7)
    tile_count = TILE_SLOTS // SLOTS
    flips = jax.random.randint(key, (SUBSETS, ANGLES, tile_count), 0, 2)
    first_side = 2 * flips - 1
    tile_index = jnp.arange(tile_count, dtype=jnp.int32)[None, None, :]
    candidates = jnp.stack([tile_index + 0 * first_side, tile_index + first_side, tile_index - first_side], axis=3)
    inside = (candidates >= 0) & (candidates < tile_count)
    chosen = jnp.where(inside, candidates, tile_index[..., None] + 0 * candidates)
    return chosen.reshape(SUBSETS, ANGLES, TILE_SLOTS).astype(jnp.int32)


def place_ends(entries, key, least, top_value):
    longest = entries.shape.index(max(entries.shape))
    spots = []
    for shift in (0, 1):
        where = [jax.random.randint(jax.random.fold_in(key, axis), (), 0, length) for axis, length in enumerate(entries.shape)]
        where[longest] = (where[longest] + shift) % entries.shape[longest]
        spots.append(tuple(where))
    return entries.at[spots[0]].set(least).at[spots[1]].set(top_value)


def block_scale(key, shape, cuts, least, high):
    def one(dim, parts):
        heights = jax.random.uniform(jax.random.fold_in(jax.random.fold_in(key, 6), dim), (parts,), jnp.float32, least / len(cuts), high / len(cuts))
        return jnp.repeat(jnp.exp(heights), shape[dim] // parts).reshape((-1,) + (1,) * (len(shape) - dim - 1))

    loudness = one(*cuts[0])
    for cut in cuts[1:]:
        loudness = loudness * one(*cut)
    return loudness


def gaussian(key, shape, scale, most, pieces=(), kind=jnp.bfloat16):
    values = scale * jax.random.normal(key, shape, jnp.float32)
    if pieces:
        values = values * block_scale(key, shape, pieces, -0.22, 0.18)
    return jnp.clip(values, -most, most).astype(kind)


def setup_inputs(seed: int = 0) -> dict:
    splits = jax.random.split(jax.random.key(seed), 6)
    return {
        "volume": gaussian(splits[0], (NZ, NX, CY), 1.0, 6.0, ((1, 32),), jnp.float32),
        "measured": gaussian(splits[1], (SUBSETS, ANGLES, RAYS, CELLS), 256.0, 1536.0, ((1, 4), (2, 32)), jnp.float32),
        "blocks": jnp.clip(0.1 + 0.9 * jax.random.uniform(splits[2], (SUBSETS, ANGLES, TILE_SLOTS, DR, NZ), jnp.float32) ** block_scale(splits[2], (SUBSETS, ANGLES, TILE_SLOTS, DR, NZ), ((1, 4), (2, 32)), -0.2, 0.2), 0.1, 1.0),
        "ray_lists": draw_ray_lists(jax.random.fold_in(splits[5], 71), 0),
        "counts": place_ends(jax.random.randint(splits[4], (SUBSETS, ANGLES, N_TILE), 1, 4), jax.random.fold_in(splits[4], 1), 1, 3).astype(jnp.int32),
    }


RELAX = 1.0
TV_WEIGHT = 0.05
TV_EPSILON = 0.01

def direction_term(volume, axis_pos):
    extent = volume.shape[axis_pos]
    edge_layer = lax.slice_in_dim(volume, extent - 1, extent, axis=axis_pos)
    ahead_layers = jnp.concatenate([lax.slice_in_dim(volume, 1, extent, axis=axis_pos), edge_layer], axis=axis_pos)
    difference = ahead_layers - volume
    fluxes = difference / jnp.sqrt(difference * difference + TV_EPSILON)
    behind = jnp.concatenate([jnp.zeros_like(edge_layer), lax.slice_in_dim(fluxes, 0, extent - 1, axis=axis_pos)], axis=axis_pos)
    return behind - fluxes

def smooth_step(volume):
    total_term = direction_term(volume, 0) + direction_term(volume, 1) + direction_term(volume, 2)
    return volume - TV_WEIGHT * total_term

def sart_subset(volume, blocks, ray_lists, counts, measured):
    tile_stack = volume.reshape(NZ, N_TILE, CX, CY).transpose(1, 0, 2, 3).reshape(N_TILE, NZ, CX * CY)
    weights = blocks.reshape(ANGLES, N_TILE, SLOTS, DR, NZ)
    ray_ids = ray_lists.reshape(ANGLES, N_TILE, SLOTS).astype(jnp.int32)
    live_slots = (jnp.arange(SLOTS, dtype=jnp.int32)[None, None, :] < counts[:, :, None]).astype(jnp.float32)
    observed = measured.reshape(ANGLES, N_TILE, DR, CX * CY)

    def one_angle(running, inputs):
        update, column_sums = running
        angle_weights, angle_ids, angle_live, angle_observed = inputs
        live_weights = angle_weights * angle_live[:, :, None, None]
        contributions = jnp.einsum('tkdz,tzc->tkdc', live_weights, tile_stack, precision=lax.Precision.HIGHEST)
        forward = jnp.zeros((N_TILE, DR, CX * CY), jnp.float32).at[angle_ids].add(contributions)
        row_sums = jnp.zeros((N_TILE, DR), jnp.float32).at[angle_ids].add(lax.optimization_barrier(jnp.sum(live_weights, axis=3)))
        residual = (angle_observed - forward) / row_sums[:, :, None]
        picked = residual[angle_ids]
        update = update + jnp.einsum('tkdz,tkdc->tzc', live_weights, picked, precision=lax.Precision.HIGHEST)
        column_sums = column_sums + lax.optimization_barrier(jnp.sum(live_weights, axis=(1, 2)))
        return ((update, column_sums), None)
    start = (jnp.zeros((N_TILE, NZ, CX * CY), jnp.float32), jnp.zeros((N_TILE, NZ), jnp.float32))
    (update, column_sums), unused = lax.scan(one_angle, start, (weights, ray_ids, live_slots, observed))
    tile_stack = tile_stack + RELAX * update / column_sums[:, :, None]
    return tile_stack.reshape(N_TILE, NZ, CX, CY).transpose(1, 0, 2, 3).reshape(NZ, N_TILE * CX, CY)

def reference(volume, measured, blocks, ray_lists, counts):
    for subset in range(SUBSETS):
        volume = sart_subset(volume, blocks[subset], ray_lists[subset], counts[subset], measured[subset])
        volume = smooth_step(volume)
    return volume
```

```python
import jax
import jax.numpy as jnp
from jax import lax
from jax.experimental import pallas as pl
from jax.experimental.pallas import tpu as pltpu
from jax.sharding import PartitionSpec as P

TV_WEIGHT = 0.05
TV_EPSILON = 0.01
MESH = pl.DeviceIdType.MESH
BF = jnp.bfloat16
F32 = jnp.float32

NZ, CY, QX = 96, 256, 8
QC = QX * CY
NC = 4
CH = QC // NC
NK = 4
ZK = NZ // NK
NA, DR, SLOTS = 8, 16, 3
ROWS = NA * DR


def split(value):
    hi = value.astype(BF)
    lo = (value - hi.astype(F32)).astype(BF)
    return hi, lo


def left_stack(value):
    hi, lo = split(value)
    return jnp.concatenate([hi, hi, lo], axis=1)


def right_stack(value):
    hi, lo = split(value)
    return jnp.concatenate([hi, lo, hi], axis=0)


def dot(a, b):
    return jnp.dot(a, b, preferred_element_type=F32)


def flux(difference):
    return difference * lax.rsqrt(difference * difference + TV_EPSILON)


def kernel(
    vol, meas, blk, ids, cnt, out,
    vq, xb, mb, ctb, csend, csb, gst, cst, po, pp, rz, rp, rsx, sp, xu, tvh, yq,
    lsem, s_w, r_w, s_ct, r_ct, s_cs, r_cs, s_m, r_m, s_h, r_h, s_z, r_z, s_p, r_p, s_x, r_x, s_t, r_t, s_o, r_o,
):
    t = lax.axis_index("tile")
    a = lax.axis_index("angle")
    nt = lax.axis_size("tile")
    h, c = a // 2, a % 2
    sib_a, xp_a, diag_a = 2 * h + 1 - c, (a + 2) % 4, 3 - a
    right_t, left_t = (t + 1) % nt, (t + nt - 1) % nt
    sib, xp, diag = (t, sib_a), (t, xp_a), (t, diag_a)
    sides = ((right_t, a), (left_t, a))
    g = t * 4 + a
    gr, gl = (g + 1) % (nt * 4), (g + nt * 4 - 1) % (nt * 4)
    tv_sides = ((gr // 4, gr % 4), (gl // 4, gl % 4))

    def remote(src, dst, ss, rs, dev):
        return pltpu.make_async_remote_copy(
            src_ref=src, dst_ref=dst, send_sem=ss, recv_sem=rs, device_id=dev, device_id_type=MESH
        )

    def vol_in():
        return pltpu.make_async_copy(vol.at[:, pl.ds(a * QX, QX), :], vq, lsem.at[0])

    def m_cols(k, core):
        return pl.ds((2 * k + core) * QC, QC)

    def m_in(s, k):
        return pltpu.make_async_copy(
            meas.at[s, :, :, m_cols(k, c)], mb.at[s, k, pl.ds(c * NA, NA)], lsem.at[1 + 2 * s + k]
        )

    def m_sib(s, k):
        return remote(
            meas.at[s, :, :, m_cols(k, 1 - c)], mb.at[s, k, pl.ds(c * NA, NA)],
            s_m.at[s, k], r_m.at[s, k], sib,
        )

    def w_side(s, d):
        return remote(csend.at[s, d], ctb.at[a, s, 2 * d], s_w.at[s, d], r_w.at[s, d], sides[d])

    def ct_sib(s):
        return remote(ctb.at[a, s], ctb.at[a, s], s_ct.at[0, s], r_ct.at[0, s], sib)

    def ct_xp(s):
        return remote(ctb.at[a, s], ctb.at[a, s], s_ct.at[1, s], r_ct.at[1, s], xp)

    def ct_fwd(s):
        return remote(ctb.at[xp_a, s], ctb.at[xp_a, s], s_ct.at[2, s], r_ct.at[2, s], sib)

    def cs_to(i):
        return remote(csb.at[a], csb.at[a], s_cs.at[i], r_cs.at[i], (sib, xp, diag)[i])

    def halo(s, d, j):
        return remote(xb.at[s, 1, j], xb.at[s, 2 * d, j], s_h.at[s, d, j], r_h.at[s, d, j], sides[d])

    def z_own(s, d, j):
        return remote(po.at[s, 2 - 2 * d, j], rz.at[s, d, j], s_z.at[s, d, j], r_z.at[s, d, j], sides[d])

    def z_part(s, d, j):
        return remote(pp.at[s, 2 - 2 * d, j], rp.at[s, d, j], s_p.at[s, d, j], r_p.at[s, d, j], sides[d])

    def x_sum(s, j):
        return remote(sp.at[s, j], rsx.at[s, j], s_x.at[s, j], r_x.at[s, j], xp)

    def tv_side(s, d):
        src = xu.at[s, NC - 1, :, pl.ds(CH - CY, CY)] if d == 0 else xu.at[s, 0, :, pl.ds(0, CY)]
        return remote(src, tvh.at[s, d], s_t.at[s, d], r_t.at[s, d], tv_sides[d])

    def out_at(k, q):
        return out.at[pl.ds(k * ZK, ZK), pl.ds(q * QX, QX), :]

    def out_own(k):
        return pltpu.make_async_copy(yq.at[pl.ds(k * ZK, ZK)], out_at(k, a), lsem.at[5 + k])

    def out_to(i, k):
        return remote(yq.at[pl.ds(k * ZK, ZK)], out_at(k, a), s_o.at[i, k], r_o.at[i, k], (sib, xp)[i])

    def out_fwd(k):
        return remote(out_at(k, xp_a), out_at(k, xp_a), s_o.at[2, k], r_o.at[2, k], sib)

    def loop(count, body):
        def step(i, carry):
            body(i)
            return carry

        lax.fori_loop(0, count, step, 0)

    vol_in().start()
    for s in range(2):
        for k in range(2):
            m_in(s, k).start()
    peers = (sib, xp, diag) + sides + tv_sides
    barrier = pltpu.get_barrier_semaphore()
    for peer in peers:
        pl.semaphore_signal(barrier, inc=1, device_id=peer, device_id_type=MESH)

    for s in range(2):
        sums = jnp.zeros((1, NZ), F32)
        for o in range(3):
            rows = []
            for n in range(NA):
                block = jnp.zeros((DR, NZ), F32)
                for k in range(SLOTS):
                    live = (cnt[s, n, 0] > k) & (ids[s, n, k] - t == o - 1)
                    block = block + blk[s, n, k] * jnp.where(live, 1.0, 0.0).astype(F32)
                rows.append(block)
            block = jnp.concatenate(rows, axis=0)
            sums = sums + jnp.sum(block, axis=0, keepdims=True)
            turned = block.T
            if o == 1:
                ctb[a, s, 1] = turned
            else:
                csend[s, 1 - o // 2] = turned
        csb[a, s] = jnp.broadcast_to(jnp.concatenate([sums, jnp.ones((1, 128 - NZ), F32)], axis=1), (8, 128))

    pl.semaphore_wait(barrier, len(peers))

    for d in range(2):
        w_side(0, d).start()
    for k in range(2):
        m_sib(0, k).start()
    for i in range(3):
        cs_to(i).start()
    vol_in().wait()
    for x in range(QX):
        xb[0, 1, x * CY // CH, :, pl.ds(x * CY % CH, CY)] = vq[:, x, :]
    for j in range(NC):
        for d in range(2):
            halo(0, d, j).start()
    for d in range(2):
        w_side(1, d).start()
    for k in range(2):
        m_sib(1, k).start()

    def weights_on(s):
        for d in range(2):
            w_side(s, d).wait_recv()
        ct_sib(s).start()
        ct_xp(s).start()

    def back_data(s):
        ct_sib(s).wait_recv()
        for k in range(2):
            m_in(s, k).wait()
            m_sib(s, k).wait_recv()
        ct = jnp.concatenate(
            [ctb[2 * h + k, s].reshape(3 * NZ, ROWS) for k in range(2)], axis=1
        )
        cst[s] = left_stack(ct / jnp.sum(ct, axis=0, keepdims=True))

        def chunk(j):
            cols = pl.ds(pl.multiple_of(j * CH, CH), CH)
            for k, target in ((1 - h, pp), (h, po)):
                rows = mb[s, k, :, :, cols].reshape(2 * ROWS, CH)
                prod = dot(cst[s], right_stack(rows))
                for o in range(3):
                    target[s, o, j] = prod[o * NZ:(o + 1) * NZ]
                if target is pp:
                    for d in range(2):
                        z_part(s, d, j).start()

        loop(NC, chunk)

    def operator(s):
        ct_xp(s).wait_recv()
        ct_fwd(s).start()
        ct_fwd(s).wait_recv()
        ct = jnp.concatenate([ctb[q, s].reshape(3 * NZ, ROWS) for q in range(4)], axis=1)
        scaled = ct / jnp.sum(ct, axis=0, keepdims=True)
        gram = lax.dot_general(
            scaled, ct, (((1,), (1,)), ((), ())),
            precision=lax.Precision.HIGHEST, preferred_element_type=F32,
        )
        gst[s] = left_stack(gram)

    def own_chunk(s, j):
        for d in range(2):
            halo(s, d, j).wait_recv()
        prod = dot(gst[s], right_stack(xb[s, :, j].reshape(3 * NZ, CH)))
        for o in range(3):
            po[s, o, j] = po[s, o, j] - prod[o * NZ:(o + 1) * NZ]
        for d in range(2):
            z_own(s, d, j).start()

    def part_chunk(s, j):
        for d in range(2):
            z_part(s, d, j).wait_recv()
        sp[s, j] = pp[s, 1, j] + rp[s, 0, j] + rp[s, 1, j]
        x_sum(s, j).start()

    def scale(s):
        sums = csb[0, s] + csb[1, s] + csb[2, s] + csb[3, s]
        square = jnp.broadcast_to(sums[:1], (128, 128)).T[:NZ]
        return 1.0 / square

    def update_chunk(s, j, inverse):
        for d in range(2):
            z_own(s, d, j).wait_recv()
        x_sum(s, j).wait_recv()
        total = po[s, 1, j] + rz[s, 0, j] + rz[s, 1, j] + rsx[s, j]
        xu[s, j] = xb[s, 1, j] + total * jnp.concatenate([inverse] * (CH // 128), axis=1)

    z_pos = lax.broadcasted_iota(jnp.int32, (NZ, CY), 0)
    y_pos = lax.broadcasted_iota(jnp.int32, (NZ, CY), 1)

    def inner_term(cur, axis, pos):
        extent = cur.shape[axis]
        ahead = pltpu.roll(cur, extent - 1, axis)
        f = flux(jnp.where(pos == extent - 1, 0.0, ahead - cur))
        return pltpu.roll(f, 1, axis) - f

    def x_row(s, x):
        return xu[s, x * CY // CH, :, pl.ds(x * CY % CH, CY)]

    def smooth(s, store):
        for d in range(2):
            tv_side(s, d).wait_recv()
        first, last = x_row(s, 0), x_row(s, QX - 1)
        left = jnp.where(g == 0, first, tvh[s, 0])
        right = jnp.where(g == nt * 4 - 1, last, tvh[s, 1])
        before = flux(first - left)
        for x in range(QX):
            cur = x_row(s, x)
            ahead = x_row(s, x + 1) if x < QX - 1 else right
            after = flux(ahead - cur)
            term = (before - after) + inner_term(cur, 0, z_pos) + inner_term(cur, 1, y_pos)
            store(x, cur - TV_WEIGHT * term)
            before = after

    def store_next(x, value):
        j = x * CY // CH
        xb[1, 1, j, :, pl.ds(x * CY % CH, CY)] = value
        if (x + 1) * CY % CH == 0:
            for d in range(2):
                halo(1, d, j).start()

    def store_last(x, value):
        yq[:, x, :] = value

    weights_on(0)
    back_data(0)
    operator(0)

    def both(j):
        own_chunk(0, j)
        part_chunk(0, j)

    loop(NC, both)
    weights_on(1)
    back_data(1)
    operator(1)
    for i in range(3):
        cs_to(i).wait_recv()
    inverse = scale(0)
    for j in (0, NC - 1, *range(1, NC - 1)):
        update_chunk(0, j, inverse)
        if j == 0:
            tv_side(0, 1).start()
        if j == NC - 1:
            tv_side(0, 0).start()
    smooth(0, store_next)

    loop(NC, lambda j: part_chunk(1, j))
    loop(NC, lambda j: own_chunk(1, j))
    inverse = scale(1)
    for j in (0, NC - 1, *range(1, NC - 1)):
        update_chunk(1, j, inverse)
        if j == 0:
            tv_side(1, 1).start()
        if j == NC - 1:
            tv_side(1, 0).start()
    smooth(1, store_last)

    for k in range(NK):
        out_to(1, k).start()
    for k in range(NK):
        out_to(0, k).start()
        out_own(k).start()
    for k in range(NK):
        out_to(1, k).wait_recv()
        out_fwd(k).start()
    for k in range(NK):
        out_to(0, k).wait_recv()
        out_fwd(k).wait_recv()
        out_own(k).wait()
        out_fwd(k).wait_send()
        for i in range(2):
            out_to(i, k).wait_send()

    for s in range(2):
        for d in range(2):
            w_side(s, d).wait_send()
            tv_side(s, d).wait_send()
        for k in range(2):
            m_sib(s, k).wait_send()
        ct_sib(s).wait_send()
        ct_xp(s).wait_send()
        ct_fwd(s).wait_send()

        def drain(j, s=s):
            for d in range(2):
                halo(s, d, j).wait_send()
                z_own(s, d, j).wait_send()
                z_part(s, d, j).wait_send()
            x_sum(s, j).wait_send()

        loop(NC, drain)
    for i in range(3):
        cs_to(i).wait_send()


def per_device(volume, measured, blocks, ray_lists, counts):
    vmem, smem, anywhere = (
        pl.BlockSpec(memory_space=space) for space in (pltpu.VMEM, pltpu.SMEM, pl.ANY)
    )
    dma = pltpu.SemaphoreType.DMA
    return pl.pallas_call(
        kernel,
        out_shape=jax.ShapeDtypeStruct(volume.shape, F32),
        in_specs=[anywhere, anywhere, vmem, smem, smem],
        out_specs=anywhere,
        scratch_shapes=[
            pltpu.VMEM((NZ, QX, CY), F32),
            pltpu.VMEM((2, 3, NC, NZ, CH), F32),
            pltpu.VMEM((2, 2, 2 * NA, DR, QC), F32),
            pltpu.VMEM((4, 2, 3, NZ, ROWS), F32),
            pltpu.VMEM((2, 2, NZ, ROWS), F32),
            pltpu.VMEM((4, 2, 8, 128), F32),
            pltpu.VMEM((2, 3 * NZ, 9 * NZ), BF),
            pltpu.VMEM((2, 3 * NZ, 6 * ROWS), BF),
            pltpu.VMEM((2, 3, NC, NZ, CH), F32),
            pltpu.VMEM((2, 3, NC, NZ, CH), F32),
            pltpu.VMEM((2, 2, NC, NZ, CH), F32),
            pltpu.VMEM((2, 2, NC, NZ, CH), F32),
            pltpu.VMEM((2, NC, NZ, CH), F32),
            pltpu.VMEM((2, NC, NZ, CH), F32),
            pltpu.VMEM((2, NC, NZ, CH), F32),
            pltpu.VMEM((2, 2, NZ, CY), F32),
            pltpu.VMEM((NZ, QX, CY), F32),
            dma((5 + NK,)),
            dma((2, 2)), dma((2, 2)),
            dma((3, 2)), dma((3, 2)),
            dma((3,)), dma((3,)),
            dma((2, 2)), dma((2, 2)),
            dma((2, 2, NC)), dma((2, 2, NC)),
            dma((2, 2, NC)), dma((2, 2, NC)),
            dma((2, 2, NC)), dma((2, 2, NC)),
            dma((2, NC)), dma((2, NC)),
            dma((2, 2)), dma((2, 2)),
            dma((3, NK)), dma((3, NK)),
        ],
        compiler_params=pltpu.CompilerParams(
            collective_id=0, has_side_effects=True, vmem_limit_bytes=56 * 1024 * 1024
        ),
        name="sart_tv",
    )(volume, measured, blocks, ray_lists, counts)


def solution(mesh):
    return jax.shard_map(
        per_device,
        mesh=mesh,
        in_specs=(
            P(None, "tile", None),
            P(None, "angle", "tile", None),
            P(None, "angle", "tile", None, None),
            P(None, "angle", "tile"),
            P(None, "angle", "tile"),
        ),
        out_specs=P(None, "tile", None),
        check_vma=False,
    )
```

```python
import jax
import jax.numpy as jnp
from jax import lax
from jax.experimental import pallas as pl
from jax.experimental.pallas import tpu as pltpu
from jax.sharding import PartitionSpec as P

TV_WEIGHT = 0.05
TV_EPSILON = 0.01
MESH = pl.DeviceIdType.MESH
BF = jnp.bfloat16
F32 = jnp.float32

NZ, CY, TX = 96, 256, 32
UX = 4
UC = UX * CY
NC = 4
CH = 2 * UC // NC
UNC = NC // 2
EARLY = 2
RUN = 4
NA, DR, SLOTS = 8, 16, 3
ROWS = NA * DR


def split(value):
    hi = value.astype(BF)
    lo = (value - hi.astype(F32)).astype(BF)
    return hi, lo


def left_stack(value):
    hi, lo = split(value)
    return jnp.concatenate([hi, hi, lo], axis=1)


def right_stack(value):
    hi, lo = split(value)
    return jnp.concatenate([hi, lo, hi], axis=0)


def dot(a, b):
    return jnp.dot(a, b, preferred_element_type=F32)


def flux(difference):
    return difference * lax.rsqrt(difference * difference + TV_EPSILON)


def kernel(
    vol, meas, blk, ids, cnt, out,
    vq, xb, mb, ctb, csend, csb, gst, cst, po, pp, rz, rp, rsx, sp, xu, tvh, xall, edge, yt,
    lsem, s_w, r_w, s_ct, r_ct, s_cs, r_cs, s_m, r_m, s_h, r_h, s_z, r_z, s_p, r_p, s_x, r_x, s_t, r_t, s_o, r_o, s_e, r_e,
):
    t = lax.axis_index("tile")
    a = lax.axis_index("angle")
    nt = lax.axis_size("tile")
    h, c = a // 2, a % 2
    sib_a, xp_a, diag_a = 2 * h + 1 - c, (a + 2) % 4, 3 - a
    right_t, left_t = (t + 1) % nt, (t + nt - 1) % nt
    sib, xp, diag = (t, sib_a), (t, xp_a), (t, diag_a)
    ends = ((t % RUN) // (RUN - 1), ((t + RUN - 1) % RUN) // (RUN - 1))
    x_lo = (t // RUN) % 2
    x_lo_left = (left_t // RUN) % 2

    def upper(angle, u):
        return (u + angle) % 2

    def side(d, u=None):
        turn = 0 if u is None else 2 * upper(a, u) * ends[d]
        return ((right_t, left_t)[d], (a + turn) % 4)

    def region(angle, u):
        up = upper(angle, u)
        return (1 - up) * angle + up * (4 + (angle + 2 * x_lo) % 4)

    b = (a + 2 * x_lo) % 4
    top, low = a // 3, 1 - (a + 3) // 4
    top_b, low_b = b // 3, 1 - (b + 3) // 4
    owners = (
        (
            (t, (1 - top) * ((a + 1) % 4) + top * (2 * x_lo), top),
            ((1 - top_b) * t + top_b * right_t, (1 - top_b) * ((a + 1) % 4), 1 - top_b),
        ),
        (
            ((1 - low) * t + low * left_t, (1 - low) * ((a + 3) % 4) + low * ((3 + 2 * x_lo_left) % 4), low),
            (t, (1 - low_b) * ((a + 3) % 4) + low_b * 3, 1 - low_b),
        ),
    )

    def beside(d, u):
        up = upper(a, u)
        tile, angle, there = (
            (1 - up) * low_one + up * up_one for low_one, up_one in zip(owners[d][0], owners[d][1])
        )
        return tile, angle, (there + angle) % 2

    def remote(src, dst, ss, rs, dev):
        return pltpu.make_async_remote_copy(
            src_ref=src, dst_ref=dst, send_sem=ss, recv_sem=rs, device_id=dev, device_id_type=MESH
        )

    def vol_in(u):
        rows = pl.ds(pl.multiple_of(region(a, u) // 2 * 8, 8), 8)
        return pltpu.make_async_copy(vol.at[:, rows, :], vq.at[u], lsem.at[u])

    def m_cols(angle, u):
        return pl.ds(pl.multiple_of(region(angle, u) * UC, UC), UC)

    def m_in(s, k, u):
        return pltpu.make_async_copy(
            meas.at[s, :, :, m_cols((a, xp_a)[k], u)], mb.at[s, k, u, pl.ds(c * NA, NA)],
            lsem.at[2 + 4 * s + 2 * k + u],
        )

    def m_sib(s, k, u):
        return remote(
            meas.at[s, :, :, m_cols((sib_a, diag_a)[k], u)], mb.at[s, k, u, pl.ds(c * NA, NA)],
            s_m.at[s, k, u], r_m.at[s, k, u], sib,
        )

    def w_side(s, d):
        return remote(csend.at[s, d], ctb.at[a, s, 2 * d], s_w.at[s, d], r_w.at[s, d], side(d))

    def ct_sib(s):
        return remote(ctb.at[a, s], ctb.at[a, s], s_ct.at[0, s], r_ct.at[0, s], sib)

    def ct_xp(s):
        return remote(ctb.at[a, s], ctb.at[a, s], s_ct.at[1, s], r_ct.at[1, s], xp)

    def ct_fwd(s):
        return remote(ctb.at[xp_a, s], ctb.at[xp_a, s], s_ct.at[2, s], r_ct.at[2, s], sib)

    def cs_to(i):
        return remote(csb.at[a], csb.at[a], s_cs.at[i], r_cs.at[i], (sib, xp, diag)[i])

    def halo(s, d, j):
        return remote(xb.at[s, 1, j], xb.at[s, 2 * d, j], s_h.at[s, d, j], r_h.at[s, d, j], side(d, j // UNC))

    def z_own(s, d, j):
        return remote(po.at[s, 2 - 2 * d, j], rz.at[s, d, j], s_z.at[s, d, j], r_z.at[s, d, j], side(d, j // UNC))

    def z_part(s, d, j):
        return remote(pp.at[s, 2 - 2 * d, j], rp.at[s, d, j], s_p.at[s, d, j], r_p.at[s, d, j], side(d, j // UNC))

    def x_sum(s, j):
        return remote(sp.at[s, j], rsx.at[s, j], s_x.at[s, j], r_x.at[s, j], xp)

    def tv_side(d, u):
        src = x_ref(u, UX - 1) if d == 0 else x_ref(u, 0)
        tile, angle, slot = beside(d, u)
        return remote(src, tvh.at[d, slot], s_t.at[d, u], r_t.at[d, slot], (tile, angle))

    def tv_from(d, u):
        return remote(tvh.at[d, u], tvh.at[d, u], s_t.at[d, u], r_t.at[d, u], sib)

    def x_ref(u, x):
        return xu.at[u * UNC + x * CY // CH, :, pl.ds(x * CY % CH, CY)]

    def x_row(u, x):
        return x_ref(u, x)[...]

    def whole_at(angle, j):
        return xall.at[region(angle, j // UNC), j % UNC]

    def whole_to(i, j):
        return remote(whole_at(a, j), whole_at(a, j), s_o.at[i, j], r_o.at[i, j], (sib, xp)[i])

    def whole_fwd(j):
        return remote(whole_at(xp_a, j), whole_at(xp_a, j), s_o.at[2, j], r_o.at[2, j], sib)

    def whole_ref(x):
        return xall.at[x // UX, x % UX * CY // CH, :, pl.ds(x * CY % CH, CY)]

    def edge_to(d):
        return remote(whole_ref((1 - d) * (TX - 1)), edge.at[d], s_e.at[d], r_e.at[d], side(d))

    def out_rows(k):
        rows = pl.ds(8 * k, 8)
        return pltpu.make_async_copy(yt.at[:, rows, :], out.at[:, rows, :], lsem.at[10 + k])

    def loop(count, body):
        def step(i, carry):
            body(i)
            return carry

        lax.fori_loop(0, count, step, 0)

    for u in range(2):
        vol_in(u).start()
    for s in range(2):
        for k in (1, 0):
            for u in range(2):
                m_in(s, k, u).start()
    peers = (sib, xp, diag) + tuple(side(d, u) for d in range(2) for u in range(2))
    peers = peers + tuple(beside(d, u)[:2] for d in range(2) for u in range(2))
    barrier = pltpu.get_barrier_semaphore()
    for peer in peers:
        pl.semaphore_signal(barrier, inc=1, device_id=peer, device_id_type=MESH)

    def own_weights(s):
        sums = jnp.zeros((1, NZ), F32)
        for o in range(3):
            rows = []
            for n in range(NA):
                block = jnp.zeros((DR, NZ), F32)
                for k in range(SLOTS):
                    live = (cnt[s, n, 0] > k) & (ids[s, n, k] - t == o - 1)
                    block = block + blk[s, n, k] * jnp.where(live, 1.0, 0.0).astype(F32)
                rows.append(block)
            block = jnp.concatenate(rows, axis=0)
            sums = sums + jnp.sum(block, axis=0, keepdims=True)
            turned = block.T
            if o == 1:
                ctb[a, s, 1] = turned
            else:
                csend[s, 1 - o // 2] = turned
        csb[a, s] = jnp.broadcast_to(jnp.concatenate([sums, jnp.ones((1, 128 - NZ), F32)], axis=1), (8, 128))

    def send_m(s):
        for k in (1, 0):
            for u in range(2):
                m_sib(s, k, u).start()

    def slab_in(u):
        vol_in(u).wait()
        first_row = region(a, u) % 2 * UX
        for x in range(UX):
            xb[0, 1, u * UNC + x * CY // CH, :, pl.ds(x * CY % CH, CY)] = vq[u, :, first_row + x, :]

    def send_halo(s, j):
        for d in range(2):
            halo(s, d, j).start()

    def send_weights(s):
        for d in range(2):
            w_side(s, d).start()

    own_weights(0)
    slab_in(0)
    pl.semaphore_wait(barrier, len(peers))
    send_weights(0)
    send_m(0)
    send_halo(0, 0)
    send_halo(0, 1)
    own_weights(1)
    send_weights(1)
    for i in range(3):
        cs_to(i).start()
    slab_in(1)

    def weights_on(s):
        for d in range(2):
            w_side(s, d).wait_recv()
        ct_sib(s).start()
        ct_xp(s).start()

    def back_weights(s):
        ct_sib(s).wait_recv()
        ct = jnp.concatenate(
            [ctb[2 * h + k, s].reshape(3 * NZ, ROWS) for k in range(2)], axis=1
        )
        cst[s] = left_stack(ct / jnp.sum(ct, axis=0, keepdims=True))

    def back_data(s, k):
        target = pp if k == 1 else po
        for u in range(2):
            m_in(s, k, u).wait()
            m_sib(s, k, u).wait_recv()

        def chunk(j):
            cols = pl.ds(pl.multiple_of(j % UNC * CH, CH), CH)
            rows = mb[s, k, j // UNC, :, :, cols].reshape(2 * ROWS, CH)
            prod = dot(cst[s], right_stack(rows))
            for o in range(3):
                target[s, o, j] = prod[o * NZ:(o + 1) * NZ]
            if k == 1 and s == 0:
                for d in range(2):
                    z_part(s, d, j).start()

        loop(NC, chunk)

    def send_part(s, j):
        for d in range(2):
            z_part(s, d, j).start()

    def operator(s):
        ct_xp(s).wait_recv()
        ct_fwd(s).start()
        ct_fwd(s).wait_recv()
        ct = jnp.concatenate([ctb[q, s].reshape(3 * NZ, ROWS) for q in range(4)], axis=1)
        scaled = ct / jnp.sum(ct, axis=0, keepdims=True)
        gram = lax.dot_general(
            scaled, ct, (((1,), (1,)), ((), ())),
            precision=lax.Precision.HIGHEST, preferred_element_type=F32,
        )
        gst[s] = left_stack(gram)

    def own_chunk(s, j):
        for d in range(2):
            halo(s, d, j).wait_recv()
        prod = dot(gst[s], right_stack(xb[s, :, j].reshape(3 * NZ, CH)))
        for o in range(3):
            po[s, o, j] = po[s, o, j] - prod[o * NZ:(o + 1) * NZ]
        for d in range(2):
            z_own(s, d, j).start()

    def part_chunk(s, j):
        for d in range(2):
            z_part(s, d, j).wait_recv()
        sp[s, j] = pp[s, 1, j] + rp[s, 0, j] + rp[s, 1, j]
        x_sum(s, j).start()

    def scale(s):
        sums = csb[0, s] + csb[1, s] + csb[2, s] + csb[3, s]
        square = jnp.broadcast_to(sums[:1], (128, 128)).T[:NZ]
        return 1.0 / square

    def update_chunk(s, j, inverse):
        for d in range(2):
            z_own(s, d, j).wait_recv()
        x_sum(s, j).wait_recv()
        total = po[s, 1, j] + rz[s, 0, j] + rz[s, 1, j] + rsx[s, j]
        updated = xb[s, 1, j] + total * jnp.concatenate([inverse] * (CH // 128), axis=1)
        if s == 0:
            xu[j] = updated
        else:
            whole_at(a, j)[...] = updated

    z_pos = lax.broadcasted_iota(jnp.int32, (NZ, CY), 0)
    y_pos = lax.broadcasted_iota(jnp.int32, (NZ, CY), 1)

    def inner_term(cur, axis, pos):
        extent = cur.shape[axis]
        ahead = pltpu.roll(cur, extent - 1, axis)
        f = flux(jnp.where(pos == extent - 1, 0.0, ahead - cur))
        return pltpu.roll(f, 1, axis) - f

    def smooth_row(cur, left, right):
        term = flux(cur - left) - flux(right - cur) + inner_term(cur, 0, z_pos) + inner_term(cur, 1, y_pos)
        return cur - TV_WEIGHT * term

    def store_next(u, x, left, right):
        j = u * UNC + x * CY // CH
        xb[1, 1, j, :, pl.ds(x * CY % CH, CY)] = smooth_row(x_row(u, x), left, right)

    def first_step():
        inverse = scale(0)
        for j in range(NC):
            update_chunk(0, j, inverse)
            if j % UNC == 0:
                tv_side(1, j // UNC).start()
            else:
                tv_side(0, j // UNC).start()
        for j in range(EARLY, NC):
            send_part(1, j)
        for u in range(2):
            for x in range(1, UX - 1):
                store_next(u, x, x_row(u, x - 1), x_row(u, x + 1))
        for j in range(EARLY):
            part_chunk(1, j)
        for j in range(NC):
            u, x = j // UNC, j % UNC * (UX - 1)
            d = 0 if x == 0 else 1
            tv_from(d, u).wait_recv()
            cur, rim = x_row(u, x), tvh[d, u]
            if d == 0:
                rim = jnp.where((t == 0) & (region(a, u) == 0), cur, rim)
                store_next(u, x, rim, x_row(u, x + 1))
            else:
                rim = jnp.where((t == nt - 1) & (region(a, u) == 7), cur, rim)
                store_next(u, x, x_row(u, x - 1), rim)
            send_halo(1, j)

    def whole_row(x):
        return whole_ref(x)[...]

    def whole_here(j):
        whole_to(0, j).wait_recv()
        whole_fwd(j).wait_recv()

    def last_row(x):
        cur = whole_row(x)
        left = whole_row(x - 1) if x > 0 else jnp.where(t == 0, cur, edge[0])
        right = whole_row(x + 1) if x < TX - 1 else jnp.where(t == nt - 1, cur, edge[1])
        yt[:, x, :] = smooth_row(cur, left, right)

    def last_step():
        inverse = scale(1)

        def pass_on(j):
            whole_to(1, j).wait_recv()
            whole_fwd(j).start()

        def update(j):
            update_chunk(1, j, inverse)
            whole_to(1, j).start()
            whole_to(0, j).start()

        done = set()

        def rows_of(first):
            for x in range(first * UX, first * UX + UX):
                if x not in done and all(
                    n in (-1, TX) or (n // UX) in ready for n in (x - 1, x + 1)
                ):
                    done.add(x)
                    last_row(x)
            k = first * UX // 8
            if all(x in done for x in range(8 * k, 8 * k + 8)):
                out_rows(k).start()

        update(0)
        update(1)
        pass_on(0)
        update(2)
        pass_on(1)
        whole_here(0)
        edge_to(1).start()
        whole_here(1)
        edge_to(0).start()
        update(3)
        pass_on(2)
        ready = (0, 2, 5, 7)
        for d in range(2):
            edge_to(d).wait_recv()
        for e in ready:
            rows_of(e)
        pass_on(3)
        for j in range(UNC, NC):
            whole_here(j)
        ready = range(TX // UX)
        for e in ready:
            rows_of(e)

    weights_on(0)
    back_weights(0)
    back_data(0, 1)
    send_halo(0, 2)
    send_halo(0, 3)
    send_m(1)
    back_data(0, 0)
    weights_on(1)
    operator(0)
    for j in range(UNC):
        part_chunk(0, j)
        own_chunk(0, j)
    for j in range(UNC, NC):
        part_chunk(0, j)
    for j in range(UNC, NC):
        own_chunk(0, j)
    back_weights(1)
    back_data(1, 1)
    for j in range(EARLY):
        send_part(1, j)
    back_data(1, 0)
    operator(1)
    for i in range(3):
        cs_to(i).wait_recv()
    first_step()

    for j in range(EARLY, NC):
        part_chunk(1, j)
    loop(NC, lambda j: own_chunk(1, j))
    last_step()

    for k in range(TX // 8):
        out_rows(k).wait()
    for j in range(NC):
        whole_fwd(j).wait_send()
        for i in range(2):
            whole_to(i, j).wait_send()
    for d in range(2):
        edge_to(d).wait_send()
        for u in range(2):
            tv_side(d, u).wait_send()
    for s in range(2):
        for d in range(2):
            w_side(s, d).wait_send()
        for k in range(2):
            for u in range(2):
                m_sib(s, k, u).wait_send()
        ct_sib(s).wait_send()
        ct_xp(s).wait_send()
        ct_fwd(s).wait_send()

        def drain(j, s=s):
            for d in range(2):
                halo(s, d, j).wait_send()
                z_own(s, d, j).wait_send()
                z_part(s, d, j).wait_send()
            x_sum(s, j).wait_send()

        loop(NC, drain)
    for i in range(3):
        cs_to(i).wait_send()


def per_device(volume, measured, blocks, ray_lists, counts):
    vmem, smem, anywhere = (
        pl.BlockSpec(memory_space=space) for space in (pltpu.VMEM, pltpu.SMEM, pl.ANY)
    )
    dma = pltpu.SemaphoreType.DMA
    return pl.pallas_call(
        kernel,
        out_shape=jax.ShapeDtypeStruct(volume.shape, F32),
        in_specs=[anywhere, anywhere, vmem, smem, smem],
        out_specs=anywhere,
        scratch_shapes=[
            pltpu.VMEM((2, NZ, 8, CY), F32),
            pltpu.VMEM((2, 3, NC, NZ, CH), F32),
            pltpu.VMEM((2, 2, 2, 2 * NA, DR, UC), F32),
            pltpu.VMEM((4, 2, 3, NZ, ROWS), F32),
            pltpu.VMEM((2, 2, NZ, ROWS), F32),
            pltpu.VMEM((4, 2, 8, 128), F32),
            pltpu.VMEM((2, 3 * NZ, 9 * NZ), BF),
            pltpu.VMEM((2, 3 * NZ, 6 * ROWS), BF),
            pltpu.VMEM((2, 3, NC, NZ, CH), F32),
            pltpu.VMEM((2, 3, NC, NZ, CH), F32),
            pltpu.VMEM((2, 2, NC, NZ, CH), F32),
            pltpu.VMEM((2, 2, NC, NZ, CH), F32),
            pltpu.VMEM((2, NC, NZ, CH), F32),
            pltpu.VMEM((2, NC, NZ, CH), F32),
            pltpu.VMEM((NC, NZ, CH), F32),
            pltpu.VMEM((2, 2, NZ, CY), F32),
            pltpu.VMEM((TX // UX, UNC, NZ, CH), F32),
            pltpu.VMEM((2, NZ, CY), F32),
            pltpu.VMEM((NZ, TX, CY), F32),
            dma((10 + TX // 8,)),
            dma((2, 2)), dma((2, 2)),
            dma((3, 2)), dma((3, 2)),
            dma((3,)), dma((3,)),
            dma((2, 2, 2)), dma((2, 2, 2)),
            dma((2, 2, NC)), dma((2, 2, NC)),
            dma((2, 2, NC)), dma((2, 2, NC)),
            dma((2, 2, NC)), dma((2, 2, NC)),
            dma((2, NC)), dma((2, NC)),
            dma((2, 2)), dma((2, 2)),
            dma((3, NC)), dma((3, NC)),
            dma((2,)), dma((2,)),
        ],
        compiler_params=pltpu.CompilerParams(
            collective_id=0, has_side_effects=True, vmem_limit_bytes=56 * 1024 * 1024
        ),
        name="sart_tv",
    )(volume, measured, blocks, ray_lists, counts)


def solution(mesh):
    return jax.shard_map(
        per_device,
        mesh=mesh,
        in_specs=(
            P(None, "tile", None),
            P(None, "angle", "tile", None),
            P(None, "angle", "tile", None, None),
            P(None, "angle", "tile"),
            P(None, "angle", "tile"),
        ),
        out_specs=P(None, "tile", None),
        check_vma=False,
    )
```

```python
import jax
import jax.numpy as jnp
from jax import lax
from jax.experimental import pallas as pl
from jax.experimental.pallas import tpu as pltpu
from jax.sharding import PartitionSpec as P

TV_WEIGHT = 0.05
TV_EPSILON = 0.01
MESH = pl.DeviceIdType.MESH
BF = jnp.bfloat16
F32 = jnp.float32

NZ, CY, TX = 96, 256, 32
UX = 4
UC = UX * CY
NC = 4
CH = 2 * UC // NC
UNC = NC // 2
EARLY = 2
RELAY = (0, 1)
RUN = 4
NA, DR, SLOTS = 8, 16, 3
ROWS = NA * DR


def split(value):
    hi = value.astype(BF)
    lo = (value - hi.astype(F32)).astype(BF)
    return hi, lo


def left_stack(value):
    hi, lo = split(value)
    return jnp.concatenate([hi, hi, lo], axis=1)


def right_stack(value):
    hi, lo = split(value)
    return jnp.concatenate([hi, lo, hi], axis=0)


def dot(a, b):
    return jnp.dot(a, b, preferred_element_type=F32)


def flux(difference):
    return difference * lax.rsqrt(difference * difference + TV_EPSILON)


def kernel(
    vol, meas, blk, lists, out,
    vq, xb, mb, ctb, csend, csb, gst, cst, po, pp, rz, rp, rsx, rly, sp, xu, tvh, xall, edge, yt,
    lsem, s_w, r_w, s_ct, r_ct, s_cs, r_cs, s_m, r_m, s_h, r_h, s_z, r_z, s_p, r_p, s_x, r_x, s_y, r_y, s_v, s_t, r_t, s_o, r_o, s_e, r_e,
):
    t = lax.axis_index("tile")
    a = lax.axis_index("angle")
    nt = lax.axis_size("tile")
    h, c = a // 2, a % 2
    sib_a, xp_a, diag_a = 2 * h + 1 - c, (a + 2) % 4, 3 - a
    right_t, left_t = (t + 1) % nt, (t + nt - 1) % nt
    sib, xp, diag = (t, sib_a), (t, xp_a), (t, diag_a)
    ends = ((t % RUN) // (RUN - 1), ((t + RUN - 1) % RUN) // (RUN - 1))
    x_lo = (t // RUN) % 2
    x_lo_left = (left_t // RUN) % 2

    def upper(angle, u):
        return (u + angle) % 2

    def side(d, u=None):
        turn = 0 if u is None else 2 * upper(a, u) * ends[d]
        return ((right_t, left_t)[d], (a + turn) % 4)

    def region(angle, u):
        up = upper(angle, u)
        return (1 - up) * angle + up * (4 + (angle + 2 * x_lo) % 4)

    pair_t = t + 1 - 2 * (t % 2)
    place = t % RUN
    outer = (place == 0) | (place == RUN - 1)
    inner = (place != 0) & (place != RUN - 1)

    b = (a + 2 * x_lo) % 4
    top, low = a // 3, 1 - (a + 3) // 4
    top_b, low_b = b // 3, 1 - (b + 3) // 4
    owners = (
        (
            (t, (1 - top) * ((a + 1) % 4) + top * (2 * x_lo), top),
            ((1 - top_b) * t + top_b * right_t, (1 - top_b) * ((a + 1) % 4), 1 - top_b),
        ),
        (
            ((1 - low) * t + low * left_t, (1 - low) * ((a + 3) % 4) + low * ((3 + 2 * x_lo_left) % 4), low),
            (t, (1 - low_b) * ((a + 3) % 4) + low_b * 3, 1 - low_b),
        ),
    )

    def beside(d, u):
        up = upper(a, u)
        tile, angle, there = (
            (1 - up) * low_one + up * up_one for low_one, up_one in zip(owners[d][0], owners[d][1])
        )
        return tile, angle, (there + angle) % 2

    def remote(src, dst, ss, rs, dev):
        return pltpu.make_async_remote_copy(
            src_ref=src, dst_ref=dst, send_sem=ss, recv_sem=rs, device_id=dev, device_id_type=MESH
        )

    def vol_in(u):
        rows = pl.ds(pl.multiple_of(region(a, u) // 2 * 8, 8), 8)
        return pltpu.make_async_copy(vol.at[:, rows, :], vq.at[u], lsem.at[u])

    def m_cols(angle, u):
        return pl.ds(pl.multiple_of(region(angle, u) * UC, UC), UC)

    def m_in(s, k, u):
        return pltpu.make_async_copy(
            meas.at[s, :, :, m_cols((a, xp_a)[k], u)], mb.at[s, k, u, pl.ds(c * NA, NA)],
            lsem.at[2 + 4 * s + 2 * k + u],
        )

    def m_sib(s, k, u):
        return remote(
            meas.at[s, :, :, m_cols((sib_a, diag_a)[k], u)], mb.at[s, k, u, pl.ds(c * NA, NA)],
            s_m.at[s, k, u], r_m.at[s, k, u], sib,
        )

    def w_side(s, d):
        return remote(csend.at[s, d], ctb.at[a, s, 2 * d], s_w.at[s, d], r_w.at[s, d], side(d))

    def ct_sib(s):
        return remote(ctb.at[a, s], ctb.at[a, s], s_ct.at[0, s], r_ct.at[0, s], sib)

    def ct_xp(s):
        return remote(ctb.at[a, s], ctb.at[a, s], s_ct.at[1, s], r_ct.at[1, s], xp)

    def ct_fwd(s):
        return remote(ctb.at[xp_a, s], ctb.at[xp_a, s], s_ct.at[2, s], r_ct.at[2, s], sib)

    def cs_to(i):
        return remote(csb.at[a], csb.at[a], s_cs.at[i], r_cs.at[i], (sib, xp, diag)[i])

    def halo(s, d, j):
        return remote(xb.at[s, 1, j], xb.at[s, 2 * d, j], s_h.at[s, d, j], r_h.at[s, d, j], side(d, j // UNC))

    def z_own(s, d, j):
        return remote(po.at[s, 2 - 2 * d, j], rz.at[s, d, j], s_z.at[s, d, j], r_z.at[s, d, j], side(d, j // UNC))

    def z_part(s, d, j):
        return remote(pp.at[s, 2 - 2 * d, j], rp.at[s, d, j], s_p.at[s, d, j], r_p.at[s, d, j], side(d, j // UNC))

    def x_sum(s, j):
        return remote(sp.at[s, j], rsx.at[s, j], s_x.at[s, j], r_x.at[s, j], xp)

    def x_out(s, j):
        return remote(sp.at[s, j], rly.at[s, j], s_y.at[s, j], r_y.at[s, j], (pair_t, a))

    def x_relay(s, j):
        return remote(rly.at[s, j], rsx.at[s, j], s_v.at[s, j], r_x.at[s, j], (pair_t, xp_a))

    def tv_side(d, u):
        src = x_ref(u, UX - 1) if d == 0 else x_ref(u, 0)
        tile, angle, slot = beside(d, u)
        return remote(src, tvh.at[d, slot], s_t.at[d, u], r_t.at[d, slot], (tile, angle))

    def tv_from(d, u):
        return remote(tvh.at[d, u], tvh.at[d, u], s_t.at[d, u], r_t.at[d, u], sib)

    def x_ref(u, x):
        return xu.at[u * UNC + x * CY // CH, :, pl.ds(x * CY % CH, CY)]

    def x_row(u, x):
        return x_ref(u, x)[...]

    def whole_at(angle, j):
        return xall.at[region(angle, j // UNC), j % UNC]

    def whole_to(i, j):
        return remote(whole_at(a, j), whole_at(a, j), s_o.at[i, j], r_o.at[i, j], (sib, xp)[i])

    def whole_fwd(j):
        return remote(whole_at(xp_a, j), whole_at(xp_a, j), s_o.at[2, j], r_o.at[2, j], sib)

    def whole_ref(x):
        return xall.at[x // UX, x % UX * CY // CH, :, pl.ds(x * CY % CH, CY)]

    def edge_to(d):
        return remote(whole_ref((1 - d) * (TX - 1)), edge.at[d], s_e.at[d], r_e.at[d], side(d))

    def out_rows(k):
        rows = pl.ds(8 * k, 8)
        return pltpu.make_async_copy(yt.at[:, rows, :], out.at[:, rows, :], lsem.at[10 + k])

    def loop(count, body):
        def step(i, carry):
            body(i)
            return carry

        lax.fori_loop(0, count, step, 0)

    for u in range(2):
        vol_in(u).start()
    for s in range(2):
        for k in (1, 0):
            for u in range(2):
                m_in(s, k, u).start()
    peers = (sib, xp, diag, (pair_t, xp_a)) + tuple(side(d, u) for d in range(2) for u in range(2))
    peers = peers + tuple(beside(d, u)[:2] for d in range(2) for u in range(2))
    barrier = pltpu.get_barrier_semaphore()
    for peer in peers:
        pl.semaphore_signal(barrier, inc=1, device_id=peer, device_id_type=MESH)

    def own_weights(s):
        sums = jnp.zeros((1, NZ), F32)
        for o in range(3):
            rows = []
            for n in range(NA):
                block = jnp.zeros((DR, NZ), F32)
                for k in range(SLOTS):
                    entry = lists[s, n, k]
                    live = (entry % 4 > k) & (entry // 4 - t == o - 1)
                    block = block + blk[s, n, k] * jnp.where(live, 1.0, 0.0).astype(F32)
                rows.append(block)
            block = jnp.concatenate(rows, axis=0)
            sums = sums + jnp.sum(block, axis=0, keepdims=True)
            turned = block.T
            if o == 1:
                ctb[a, s, 1] = turned
            else:
                csend[s, 1 - o // 2] = turned
        csb[a, s] = jnp.broadcast_to(jnp.concatenate([sums, jnp.ones((1, 128 - NZ), F32)], axis=1), (8, 128))

    def send_m(s):
        for k in (1, 0):
            for u in range(2):
                m_sib(s, k, u).start()

    def slab_in(u):
        vol_in(u).wait()
        first_row = region(a, u) % 2 * UX
        for x in range(UX):
            xb[0, 1, u * UNC + x * CY // CH, :, pl.ds(x * CY % CH, CY)] = vq[u, :, first_row + x, :]

    def send_halo(s, j):
        for d in range(2):
            halo(s, d, j).start()

    def send_weights(s):
        for d in range(2):
            w_side(s, d).start()

    own_weights(0)
    slab_in(0)
    pl.semaphore_wait(barrier, len(peers))
    send_weights(0)
    send_m(0)
    send_halo(0, 0)
    send_halo(0, 1)
    own_weights(1)
    send_weights(1)
    for i in range(3):
        cs_to(i).start()
    slab_in(1)

    def weights_on(s):
        for d in range(2):
            w_side(s, d).wait_recv()
        ct_sib(s).start()
        ct_xp(s).start()

    def back_weights(s):
        ct_sib(s).wait_recv()
        ct = jnp.concatenate(
            [ctb[2 * h + k, s].reshape(3 * NZ, ROWS) for k in range(2)], axis=1
        )
        cst[s] = left_stack(ct / jnp.sum(ct, axis=0, keepdims=True))

    def back_data(s, k):
        target = pp if k == 1 else po
        for u in range(2):
            m_in(s, k, u).wait()
            m_sib(s, k, u).wait_recv()

        def chunk(j):
            cols = pl.ds(pl.multiple_of(j % UNC * CH, CH), CH)
            rows = mb[s, k, j // UNC, :, :, cols].reshape(2 * ROWS, CH)
            prod = dot(cst[s], right_stack(rows))
            for o in range(3):
                target[s, o, j] = prod[o * NZ:(o + 1) * NZ]
            if k == 1 and s == 0:
                for d in range(2):
                    z_part(s, d, j).start()

        loop(NC, chunk)

    def send_part(s, j):
        for d in range(2):
            z_part(s, d, j).start()

    def operator(s):
        ct_xp(s).wait_recv()
        ct_fwd(s).start()
        ct_fwd(s).wait_recv()
        ct = jnp.concatenate([ctb[q, s].reshape(3 * NZ, ROWS) for q in range(4)], axis=1)
        scaled = ct / jnp.sum(ct, axis=0, keepdims=True)
        gram = lax.dot_general(
            scaled, ct, (((1,), (1,)), ((), ())),
            precision=lax.Precision.HIGHEST, preferred_element_type=F32,
        )
        gst[s] = left_stack(gram)

    def own_chunk(s, j):
        for d in range(2):
            halo(s, d, j).wait_recv()
        prod = dot(gst[s], right_stack(xb[s, :, j].reshape(3 * NZ, CH)))
        for o in range(3):
            po[s, o, j] = po[s, o, j] - prod[o * NZ:(o + 1) * NZ]
        for d in range(2):
            z_own(s, d, j).start()

    def part_chunk(s, j):
        for d in range(2):
            z_part(s, d, j).wait_recv()
        sp[s, j] = pp[s, 1, j] + rp[s, 0, j] + rp[s, 1, j]
        if j not in RELAY:
            x_sum(s, j).start()
            return

        @pl.when(inner)
        def _():
            x_sum(s, j).start()

        @pl.when(outer)
        def _():
            x_out(s, j).start()

    def relay(s):
        @pl.when(inner)
        def _():
            for j in RELAY:
                x_out(s, j).wait_recv()
                x_relay(s, j).start()

    def scale(s):
        sums = csb[0, s] + csb[1, s] + csb[2, s] + csb[3, s]
        square = jnp.broadcast_to(sums[:1], (128, 128)).T[:NZ]
        return 1.0 / square

    def update_chunk(s, j, inverse):
        for d in range(2):
            z_own(s, d, j).wait_recv()
        x_sum(s, j).wait_recv()
        total = po[s, 1, j] + rz[s, 0, j] + rz[s, 1, j] + rsx[s, j]
        updated = xb[s, 1, j] + total * jnp.concatenate([inverse] * (CH // 128), axis=1)
        if s == 0:
            xu[j] = updated
        else:
            whole_at(a, j)[...] = updated

    z_pos = lax.broadcasted_iota(jnp.int32, (NZ, CY), 0)
    y_pos = lax.broadcasted_iota(jnp.int32, (NZ, CY), 1)

    def inner_term(cur, axis, pos):
        extent = cur.shape[axis]
        ahead = pltpu.roll(cur, extent - 1, axis)
        f = flux(jnp.where(pos == extent - 1, 0.0, ahead - cur))
        return pltpu.roll(f, 1, axis) - f

    def smooth_row(cur, left, right):
        term = flux(cur - left) - flux(right - cur) + inner_term(cur, 0, z_pos) + inner_term(cur, 1, y_pos)
        return cur - TV_WEIGHT * term

    def store_next(u, x, left, right):
        j = u * UNC + x * CY // CH
        xb[1, 1, j, :, pl.ds(x * CY % CH, CY)] = smooth_row(x_row(u, x), left, right)

    def first_step():
        inverse = scale(0)
        for j in range(NC):
            update_chunk(0, j, inverse)
            if j % UNC == 0:
                tv_side(1, j // UNC).start()
            else:
                tv_side(0, j // UNC).start()
        for j in range(EARLY, NC):
            send_part(1, j)
        for u in range(2):
            for x in range(1, UX - 1):
                store_next(u, x, x_row(u, x - 1), x_row(u, x + 1))
        for j in range(EARLY):
            part_chunk(1, j)
        for j in range(NC):
            u, x = j // UNC, j % UNC * (UX - 1)
            d = 0 if x == 0 else 1
            tv_from(d, u).wait_recv()
            cur, rim = x_row(u, x), tvh[d, u]
            if d == 0:
                rim = jnp.where((t == 0) & (region(a, u) == 0), cur, rim)
                store_next(u, x, rim, x_row(u, x + 1))
            else:
                rim = jnp.where((t == nt - 1) & (region(a, u) == 7), cur, rim)
                store_next(u, x, x_row(u, x - 1), rim)
            send_halo(1, j)

    def whole_row(x):
        return whole_ref(x)[...]

    def whole_here(j):
        whole_to(0, j).wait_recv()
        whole_fwd(j).wait_recv()

    def last_row(x):
        cur = whole_row(x)
        left = whole_row(x - 1) if x > 0 else jnp.where(t == 0, cur, edge[0])
        right = whole_row(x + 1) if x < TX - 1 else jnp.where(t == nt - 1, cur, edge[1])
        yt[:, x, :] = smooth_row(cur, left, right)

    def last_step():
        inverse = scale(1)

        def pass_on(j):
            whole_to(1, j).wait_recv()
            whole_fwd(j).start()

        def update(j):
            update_chunk(1, j, inverse)
            whole_to(1, j).start()
            whole_to(0, j).start()

        done = set()

        def rows_of(first):
            for x in range(first * UX, first * UX + UX):
                if x not in done and all(
                    n in (-1, TX) or (n // UX) in ready for n in (x - 1, x + 1)
                ):
                    done.add(x)
                    last_row(x)
            k = first * UX // 8
            if all(x in done for x in range(8 * k, 8 * k + 8)):
                out_rows(k).start()

        update(0)
        update(1)
        pass_on(0)
        update(2)
        pass_on(1)
        whole_here(0)
        edge_to(1).start()
        whole_here(1)
        edge_to(0).start()
        update(3)
        pass_on(2)
        ready = (0, 2, 5, 7)
        for d in range(2):
            edge_to(d).wait_recv()
        for e in ready:
            rows_of(e)
        pass_on(3)
        for j in range(UNC, NC):
            whole_here(j)
        ready = range(TX // UX)
        for e in ready:
            rows_of(e)

    weights_on(0)
    back_weights(0)
    back_data(0, 1)
    send_halo(0, 2)
    send_halo(0, 3)
    send_m(1)
    weights_on(1)
    back_data(0, 0)
    part_chunk(0, 0)
    operator(0)
    part_chunk(0, 1)
    own_chunk(0, 0)
    part_chunk(0, 2)
    own_chunk(0, 1)
    part_chunk(0, 3)
    for j in range(UNC, NC):
        own_chunk(0, j)
    back_weights(1)
    back_data(1, 1)
    relay(0)
    for j in range(EARLY):
        send_part(1, j)
    back_data(1, 0)
    operator(1)
    for i in range(3):
        cs_to(i).wait_recv()
    first_step()

    for j in range(EARLY, NC):
        part_chunk(1, j)
    for j in range(NC):
        own_chunk(1, j)
        if j == 1:
            relay(1)
    last_step()

    for k in range(TX // 8):
        out_rows(k).wait()
    for j in range(NC):
        whole_fwd(j).wait_send()
        for i in range(2):
            whole_to(i, j).wait_send()
    for d in range(2):
        edge_to(d).wait_send()
        for u in range(2):
            tv_side(d, u).wait_send()
    for s in range(2):
        for d in range(2):
            w_side(s, d).wait_send()
        for k in range(2):
            for u in range(2):
                m_sib(s, k, u).wait_send()
        ct_sib(s).wait_send()
        ct_xp(s).wait_send()
        ct_fwd(s).wait_send()

        def drain(j, s=s):
            for d in range(2):
                halo(s, d, j).wait_send()
                z_own(s, d, j).wait_send()
                z_part(s, d, j).wait_send()

        loop(NC, drain)
        for j in range(NC):
            if j not in RELAY:
                x_sum(s, j).wait_send()

        @pl.when(inner)
        def _(s=s):
            for j in RELAY:
                x_sum(s, j).wait_send()
                x_relay(s, j).wait_send()

        @pl.when(outer)
        def _(s=s):
            for j in RELAY:
                x_out(s, j).wait_send()

    for i in range(3):
        cs_to(i).wait_send()


def per_device(volume, measured, blocks, ray_lists, counts):
    vmem, smem, anywhere = (
        pl.BlockSpec(memory_space=space) for space in (pltpu.VMEM, pltpu.SMEM, pl.ANY)
    )
    lists = ray_lists * 4 + counts
    dma = pltpu.SemaphoreType.DMA
    return pl.pallas_call(
        kernel,
        out_shape=jax.ShapeDtypeStruct(volume.shape, F32),
        in_specs=[anywhere, anywhere, vmem, smem],
        out_specs=anywhere,
        scratch_shapes=[
            pltpu.VMEM((2, NZ, 8, CY), F32),
            pltpu.VMEM((2, 3, NC, NZ, CH), F32),
            pltpu.VMEM((2, 2, 2, 2 * NA, DR, UC), F32),
            pltpu.VMEM((4, 2, 3, NZ, ROWS), F32),
            pltpu.VMEM((2, 2, NZ, ROWS), F32),
            pltpu.VMEM((4, 2, 8, 128), F32),
            pltpu.VMEM((2, 3 * NZ, 9 * NZ), BF),
            pltpu.VMEM((2, 3 * NZ, 6 * ROWS), BF),
            pltpu.VMEM((2, 3, NC, NZ, CH), F32),
            pltpu.VMEM((2, 3, NC, NZ, CH), F32),
            pltpu.VMEM((2, 2, NC, NZ, CH), F32),
            pltpu.VMEM((2, 2, NC, NZ, CH), F32),
            pltpu.VMEM((2, NC, NZ, CH), F32),
            pltpu.VMEM((2, max(RELAY) + 1, NZ, CH), F32),
            pltpu.VMEM((2, NC, NZ, CH), F32),
            pltpu.VMEM((NC, NZ, CH), F32),
            pltpu.VMEM((2, 2, NZ, CY), F32),
            pltpu.VMEM((TX // UX, UNC, NZ, CH), F32),
            pltpu.VMEM((2, NZ, CY), F32),
            pltpu.VMEM((NZ, TX, CY), F32),
            dma((10 + TX // 8,)),
            dma((2, 2)), dma((2, 2)),
            dma((3, 2)), dma((3, 2)),
            dma((3,)), dma((3,)),
            dma((2, 2, 2)), dma((2, 2, 2)),
            dma((2, 2, NC)), dma((2, 2, NC)),
            dma((2, 2, NC)), dma((2, 2, NC)),
            dma((2, 2, NC)), dma((2, 2, NC)),
            dma((2, NC)), dma((2, NC)),
            dma((2, NC)), dma((2, NC)), dma((2, NC)),
            dma((2, 2)), dma((2, 2)),
            dma((3, NC)), dma((3, NC)),
            dma((2,)), dma((2,)),
        ],
        compiler_params=pltpu.CompilerParams(
            collective_id=0, has_side_effects=True, vmem_limit_bytes=50 * 1024 * 1024
        ),
        name="sart_tv",
    )(volume, measured, blocks, lists)


def solution(mesh):
    return jax.shard_map(
        per_device,
        mesh=mesh,
        in_specs=(
            P(None, "tile", None),
            P(None, "angle", "tile", None),
            P(None, "angle", "tile", None, None),
            P(None, "angle", "tile"),
            P(None, "angle", "tile"),
        ),
        out_specs=P(None, "tile", None),
        check_vma=False,
    )
```

```python
import jax
import jax.numpy as jnp
from jax import lax
from jax.experimental import pallas as pl
from jax.experimental.pallas import tpu as pltpu
from jax.sharding import PartitionSpec as P

TV_WEIGHT = 0.05
TV_EPSILON = 0.01
MESH = pl.DeviceIdType.MESH
BF = jnp.bfloat16
F32 = jnp.float32

NZ, CY, TX = 96, 256, 32
UX = 4
UC = UX * CY
NC = 4
CH = 2 * UC // NC
UNC = NC // 2
EARLY = 2
RELAY = ((0, 1), (0, 1, 2))
RUN = 4
NA, DR, SLOTS = 8, 16, 3
ROWS = NA * DR


def split(value):
    hi = value.astype(BF)
    lo = (value - hi.astype(F32)).astype(BF)
    return hi, lo


def left_stack(value):
    hi, lo = split(value)
    return jnp.concatenate([hi, hi, lo], axis=1)


def right_stack(value):
    hi, lo = split(value)
    return jnp.concatenate([hi, lo, hi], axis=0)


def dot(a, b):
    return jnp.dot(a, b, preferred_element_type=F32)


def flux(difference):
    return difference * lax.rsqrt(difference * difference + TV_EPSILON)


def kernel(
    vol, meas, blk, lists, out,
    vq, xb, mb, ctb, csend, csb, gst, cst, po, pp, rz, rp, rsx, rly, sp, xu, tvh, xall, edge, yt,
    lsem, s_w, r_w, s_ct, r_ct, s_cs, r_cs, s_m, r_m, s_h, r_h, s_z, r_z, s_p, r_p, s_x, r_x, s_y, r_y, s_v, s_t, r_t, s_o, r_o, s_e, r_e,
):
    t = lax.axis_index("tile")
    a = lax.axis_index("angle")
    nt = lax.axis_size("tile")
    h, c = a // 2, a % 2
    sib_a, xp_a, diag_a = 2 * h + 1 - c, (a + 2) % 4, 3 - a
    right_t, left_t = (t + 1) % nt, (t + nt - 1) % nt
    sib, xp, diag = (t, sib_a), (t, xp_a), (t, diag_a)
    ends = ((t % RUN) // (RUN - 1), ((t + RUN - 1) % RUN) // (RUN - 1))
    x_lo = (t // RUN) % 2
    x_lo_left = (left_t // RUN) % 2

    def upper(angle, u):
        return (u + angle) % 2

    def side(d, u=None):
        turn = 0 if u is None else 2 * upper(a, u) * ends[d]
        return ((right_t, left_t)[d], (a + turn) % 4)

    def region(angle, u):
        up = upper(angle, u)
        return (1 - up) * angle + up * (4 + (angle + 2 * x_lo) % 4)

    pair_t = t + 1 - 2 * (t % 2)
    place = t % RUN
    outer = (place == 0) | (place == RUN - 1)
    inner = (place != 0) & (place != RUN - 1)

    b = (a + 2 * x_lo) % 4
    top, low = a // 3, 1 - (a + 3) // 4
    top_b, low_b = b // 3, 1 - (b + 3) // 4
    owners = (
        (
            (t, (1 - top) * ((a + 1) % 4) + top * (2 * x_lo), top),
            ((1 - top_b) * t + top_b * right_t, (1 - top_b) * ((a + 1) % 4), 1 - top_b),
        ),
        (
            ((1 - low) * t + low * left_t, (1 - low) * ((a + 3) % 4) + low * ((3 + 2 * x_lo_left) % 4), low),
            (t, (1 - low_b) * ((a + 3) % 4) + low_b * 3, 1 - low_b),
        ),
    )

    def beside(d, u):
        up = upper(a, u)
        tile, angle, there = (
            (1 - up) * low_one + up * up_one for low_one, up_one in zip(owners[d][0], owners[d][1])
        )
        return tile, angle, (there + angle) % 2

    def remote(src, dst, ss, rs, dev):
        return pltpu.make_async_remote_copy(
            src_ref=src, dst_ref=dst, send_sem=ss, recv_sem=rs, device_id=dev, device_id_type=MESH
        )

    def vol_in(u):
        rows = pl.ds(pl.multiple_of(region(a, u) // 2 * 8, 8), 8)
        return pltpu.make_async_copy(vol.at[:, rows, :], vq.at[u], lsem.at[u])

    def m_cols(angle, u):
        return pl.ds(pl.multiple_of(region(angle, u) * UC, UC), UC)

    def m_in(s, k, u):
        return pltpu.make_async_copy(
            meas.at[s, :, :, m_cols((a, xp_a)[k], u)], mb.at[s, k, u, pl.ds(c * NA, NA)],
            lsem.at[2 + 4 * s + 2 * k + u],
        )

    def m_sib(s, k, u):
        return remote(
            meas.at[s, :, :, m_cols((sib_a, diag_a)[k], u)], mb.at[s, k, u, pl.ds(c * NA, NA)],
            s_m.at[s, k, u], r_m.at[s, k, u], sib,
        )

    def w_side(s, d):
        return remote(csend.at[s, d], ctb.at[a, s, 2 * d], s_w.at[s, d], r_w.at[s, d], side(d))

    def ct_sib(s):
        return remote(ctb.at[a, s], ctb.at[a, s], s_ct.at[0, s], r_ct.at[0, s], sib)

    def ct_xp(s):
        return remote(ctb.at[a, s], ctb.at[a, s], s_ct.at[1, s], r_ct.at[1, s], xp)

    def ct_fwd(s):
        return remote(ctb.at[xp_a, s], ctb.at[xp_a, s], s_ct.at[2, s], r_ct.at[2, s], sib)

    def cs_to(i):
        return remote(csb.at[a], csb.at[a], s_cs.at[i], r_cs.at[i], (sib, xp, diag)[i])

    def halo(s, d, j):
        return remote(xb.at[s, 1, j], xb.at[s, 2 * d, j], s_h.at[s, d, j], r_h.at[s, d, j], side(d, j // UNC))

    def z_own(s, d, j):
        return remote(po.at[s, 2 - 2 * d, j], rz.at[s, d, j], s_z.at[s, d, j], r_z.at[s, d, j], side(d, j // UNC))

    def z_part(s, d, j):
        return remote(pp.at[s, 2 - 2 * d, j], rp.at[s, d, j], s_p.at[s, d, j], r_p.at[s, d, j], side(d, j // UNC))

    def x_sum(s, j):
        return remote(sp.at[s, j], rsx.at[s, j], s_x.at[s, j], r_x.at[s, j], xp)

    def x_out(s, j):
        return remote(sp.at[s, j], rly.at[s, j], s_y.at[s, j], r_y.at[s, j], (pair_t, a))

    def x_relay(s, j):
        return remote(rly.at[s, j], rsx.at[s, j], s_v.at[s, j], r_x.at[s, j], (pair_t, xp_a))

    def tv_side(d, u):
        src = x_ref(u, UX - 1) if d == 0 else x_ref(u, 0)
        tile, angle, slot = beside(d, u)
        return remote(src, tvh.at[d, slot], s_t.at[d, u], r_t.at[d, slot], (tile, angle))

    def tv_from(d, u):
        return remote(tvh.at[d, u], tvh.at[d, u], s_t.at[d, u], r_t.at[d, u], sib)

    def x_ref(u, x):
        return xu.at[u * UNC + x * CY // CH, :, pl.ds(x * CY % CH, CY)]

    def x_row(u, x):
        return x_ref(u, x)[...]

    def whole_at(angle, j):
        return xall.at[region(angle, j // UNC), j % UNC]

    def whole_to(i, j):
        return remote(whole_at(a, j), whole_at(a, j), s_o.at[i, j], r_o.at[i, j], (sib, xp)[i])

    def whole_fwd(j):
        return remote(whole_at(xp_a, j), whole_at(xp_a, j), s_o.at[2, j], r_o.at[2, j], sib)

    def whole_ref(x):
        return xall.at[x // UX, x % UX * CY // CH, :, pl.ds(x * CY % CH, CY)]

    def edge_to(d):
        return remote(whole_ref((1 - d) * (TX - 1)), edge.at[d], s_e.at[d], r_e.at[d], side(d))

    def out_rows(k):
        rows = pl.ds(8 * k, 8)
        return pltpu.make_async_copy(yt.at[:, rows, :], out.at[:, rows, :], lsem.at[10 + k])

    def loop(count, body):
        def step(i, carry):
            body(i)
            return carry

        lax.fori_loop(0, count, step, 0)

    for u in range(2):
        vol_in(u).start()
    for s in range(2):
        for k in (1, 0):
            for u in range(2):
                m_in(s, k, u).start()
    peers = (sib, xp, diag, (pair_t, xp_a)) + tuple(side(d, u) for d in range(2) for u in range(2))
    peers = peers + tuple(beside(d, u)[:2] for d in range(2) for u in range(2))
    barrier = pltpu.get_barrier_semaphore()
    for peer in peers:
        pl.semaphore_signal(barrier, inc=1, device_id=peer, device_id_type=MESH)

    def own_weights(s):
        sums = jnp.zeros((1, NZ), F32)
        for o in range(3):
            rows = []
            for n in range(NA):
                block = jnp.zeros((DR, NZ), F32)
                for k in range(SLOTS):
                    entry = lists[s, n, k]
                    live = (entry % 4 > k) & (entry // 4 - t == o - 1)
                    block = block + blk[s, n, k] * jnp.where(live, 1.0, 0.0).astype(F32)
                rows.append(block)
            block = jnp.concatenate(rows, axis=0)
            sums = sums + jnp.sum(block, axis=0, keepdims=True)
            turned = block.T
            if o == 1:
                ctb[a, s, 1] = turned
            else:
                csend[s, 1 - o // 2] = turned
        csb[a, s] = jnp.broadcast_to(jnp.concatenate([sums, jnp.ones((1, 128 - NZ), F32)], axis=1), (8, 128))

    def send_m(s):
        for k in (1, 0):
            for u in range(2):
                m_sib(s, k, u).start()

    def slab_in(u):
        vol_in(u).wait()
        first_row = region(a, u) % 2 * UX
        for x in range(UX):
            xb[0, 1, u * UNC + x * CY // CH, :, pl.ds(x * CY % CH, CY)] = vq[u, :, first_row + x, :]

    def send_halo(s, j):
        for d in range(2):
            halo(s, d, j).start()

    def send_weights(s):
        for d in range(2):
            w_side(s, d).start()

    own_weights(0)
    slab_in(0)
    pl.semaphore_wait(barrier, len(peers))
    send_weights(0)
    send_m(0)
    send_halo(0, 0)
    send_halo(0, 1)
    own_weights(1)
    send_weights(1)
    for i in range(3):
        cs_to(i).start()
    slab_in(1)

    def weights_on(s):
        for d in range(2):
            w_side(s, d).wait_recv()
        ct_sib(s).start()
        ct_xp(s).start()

    def back_weights(s):
        ct_sib(s).wait_recv()
        ct = jnp.concatenate(
            [ctb[2 * h + k, s].reshape(3 * NZ, ROWS) for k in range(2)], axis=1
        )
        cst[s] = left_stack(ct / jnp.sum(ct, axis=0, keepdims=True))

    def back_data(s, k):
        target = pp if k == 1 else po
        for u in range(2):
            m_in(s, k, u).wait()
            m_sib(s, k, u).wait_recv()

        def chunk(j):
            cols = pl.ds(pl.multiple_of(j % UNC * CH, CH), CH)
            rows = mb[s, k, j // UNC, :, :, cols].reshape(2 * ROWS, CH)
            prod = dot(cst[s], right_stack(rows))
            for o in range(3):
                target[s, o, j] = prod[o * NZ:(o + 1) * NZ]
            if k == 1 and s == 0:
                for d in range(2):
                    z_part(s, d, j).start()

        loop(NC, chunk)

    def send_part(s, j):
        for d in range(2):
            z_part(s, d, j).start()

    def operator(s):
        ct_xp(s).wait_recv()
        ct_fwd(s).start()
        ct_fwd(s).wait_recv()
        ct = jnp.concatenate([ctb[q, s].reshape(3 * NZ, ROWS) for q in range(4)], axis=1)
        scaled = ct / jnp.sum(ct, axis=0, keepdims=True)
        gram = lax.dot_general(
            scaled, ct, (((1,), (1,)), ((), ())),
            precision=lax.Precision.HIGHEST, preferred_element_type=F32,
        )
        gst[s] = left_stack(gram)

    def own_chunk(s, j):
        for d in range(2):
            halo(s, d, j).wait_recv()
        prod = dot(gst[s], right_stack(xb[s, :, j].reshape(3 * NZ, CH)))
        for o in range(3):
            po[s, o, j] = po[s, o, j] - prod[o * NZ:(o + 1) * NZ]
        for d in range(2):
            z_own(s, d, j).start()

    def part_chunk(s, j):
        for d in range(2):
            z_part(s, d, j).wait_recv()
        sp[s, j] = pp[s, 1, j] + rp[s, 0, j] + rp[s, 1, j]
        if j not in RELAY[s]:
            x_sum(s, j).start()
            return

        @pl.when(inner)
        def _():
            x_sum(s, j).start()

        @pl.when(outer)
        def _():
            x_out(s, j).start()

    def relay_one(s, j):
        @pl.when(inner)
        def _():
            x_out(s, j).wait_recv()
            x_relay(s, j).start()

    def relay(s):
        @pl.when(inner)
        def _():
            for j in RELAY[s]:
                x_out(s, j).wait_recv()
                x_relay(s, j).start()

    def scale(s):
        sums = csb[0, s] + csb[1, s] + csb[2, s] + csb[3, s]
        square = jnp.broadcast_to(sums[:1], (128, 128)).T[:NZ]
        return 1.0 / square

    def update_chunk(s, j, inverse):
        for d in range(2):
            z_own(s, d, j).wait_recv()
        x_sum(s, j).wait_recv()
        total = po[s, 1, j] + rz[s, 0, j] + rz[s, 1, j] + rsx[s, j]
        updated = xb[s, 1, j] + total * jnp.concatenate([inverse] * (CH // 128), axis=1)
        if s == 0:
            xu[j] = updated
        else:
            whole_at(a, j)[...] = updated

    z_pos = lax.broadcasted_iota(jnp.int32, (NZ, CY), 0)
    y_pos = lax.broadcasted_iota(jnp.int32, (NZ, CY), 1)

    def inner_term(cur, axis, pos):
        extent = cur.shape[axis]
        ahead = pltpu.roll(cur, extent - 1, axis)
        f = flux(jnp.where(pos == extent - 1, 0.0, ahead - cur))
        return pltpu.roll(f, 1, axis) - f

    def smooth_row(cur, left, right):
        term = flux(cur - left) - flux(right - cur) + inner_term(cur, 0, z_pos) + inner_term(cur, 1, y_pos)
        return cur - TV_WEIGHT * term

    def store_next(u, x, left, right):
        j = u * UNC + x * CY // CH
        xb[1, 1, j, :, pl.ds(x * CY % CH, CY)] = smooth_row(x_row(u, x), left, right)

    def first_step():
        inverse = scale(0)
        for j in range(NC):
            update_chunk(0, j, inverse)
            if j % UNC == 0:
                tv_side(1, j // UNC).start()
            else:
                tv_side(0, j // UNC).start()
        for j in range(EARLY, NC):
            send_part(1, j)
        for u in range(2):
            for x in range(1, UX - 1):
                store_next(u, x, x_row(u, x - 1), x_row(u, x + 1))
        for j in range(EARLY):
            part_chunk(1, j)
        for j in range(NC):
            u, x = j // UNC, j % UNC * (UX - 1)
            d = 0 if x == 0 else 1
            tv_from(d, u).wait_recv()
            cur, rim = x_row(u, x), tvh[d, u]
            if d == 0:
                rim = jnp.where((t == 0) & (region(a, u) == 0), cur, rim)
                store_next(u, x, rim, x_row(u, x + 1))
            else:
                rim = jnp.where((t == nt - 1) & (region(a, u) == 7), cur, rim)
                store_next(u, x, x_row(u, x - 1), rim)
            send_halo(1, j)

    def whole_row(x):
        return whole_ref(x)[...]

    def whole_here(j):
        whole_to(0, j).wait_recv()
        whole_fwd(j).wait_recv()

    def last_row(x):
        cur = whole_row(x)
        left = whole_row(x - 1) if x > 0 else jnp.where(t == 0, cur, edge[0])
        right = whole_row(x + 1) if x < TX - 1 else jnp.where(t == nt - 1, cur, edge[1])
        yt[:, x, :] = smooth_row(cur, left, right)

    def last_step():
        inverse = scale(1)

        def pass_on(j):
            whole_to(1, j).wait_recv()
            whole_fwd(j).start()

        def update(j):
            update_chunk(1, j, inverse)
            whole_to(1, j).start()
            whole_to(0, j).start()

        done = set()

        def rows_of(first):
            for x in range(first * UX, first * UX + UX):
                if x not in done and all(
                    n in (-1, TX) or (n // UX) in ready for n in (x - 1, x + 1)
                ):
                    done.add(x)
                    last_row(x)
            k = first * UX // 8
            if all(x in done for x in range(8 * k, 8 * k + 8)):
                out_rows(k).start()

        update(0)
        update(1)
        pass_on(0)
        update(2)
        pass_on(1)
        whole_here(0)
        edge_to(1).start()
        whole_here(1)
        edge_to(0).start()
        update(3)
        pass_on(2)
        ready = (0, 2, 5, 7)
        for d in range(2):
            edge_to(d).wait_recv()
        for e in ready:
            rows_of(e)
        pass_on(3)
        for j in range(UNC, NC):
            whole_here(j)
        ready = range(TX // UX)
        for e in ready:
            rows_of(e)

    weights_on(0)
    back_weights(0)
    back_data(0, 1)
    send_halo(0, 2)
    send_halo(0, 3)
    send_m(1)
    weights_on(1)
    back_data(0, 0)
    part_chunk(0, 0)
    operator(0)
    part_chunk(0, 1)
    own_chunk(0, 0)
    part_chunk(0, 2)
    own_chunk(0, 1)
    part_chunk(0, 3)
    for j in range(UNC, NC):
        own_chunk(0, j)
    back_weights(1)
    back_data(1, 1)
    relay(0)
    for j in range(EARLY):
        send_part(1, j)
    back_data(1, 0)
    operator(1)
    for i in range(3):
        cs_to(i).wait_recv()
    first_step()

    for j in range(EARLY, NC):
        part_chunk(1, j)
    for j in range(NC):
        own_chunk(1, j)
        if j in RELAY[1]:
            relay_one(1, j)
    last_step()

    for k in range(TX // 8):
        out_rows(k).wait()
    for j in range(NC):
        whole_fwd(j).wait_send()
        for i in range(2):
            whole_to(i, j).wait_send()
    for d in range(2):
        edge_to(d).wait_send()
        for u in range(2):
            tv_side(d, u).wait_send()
    for s in range(2):
        for d in range(2):
            w_side(s, d).wait_send()
        for k in range(2):
            for u in range(2):
                m_sib(s, k, u).wait_send()
        ct_sib(s).wait_send()
        ct_xp(s).wait_send()
        ct_fwd(s).wait_send()

        def drain(j, s=s):
            for d in range(2):
                halo(s, d, j).wait_send()
                z_own(s, d, j).wait_send()
                z_part(s, d, j).wait_send()

        loop(NC, drain)
        for j in range(NC):
            if j not in RELAY[s]:
                x_sum(s, j).wait_send()

        @pl.when(inner)
        def _(s=s):
            for j in RELAY[s]:
                x_sum(s, j).wait_send()
                x_relay(s, j).wait_send()

        @pl.when(outer)
        def _(s=s):
            for j in RELAY[s]:
                x_out(s, j).wait_send()

    for i in range(3):
        cs_to(i).wait_send()


def per_device(volume, measured, blocks, ray_lists, counts):
    vmem, smem, anywhere = (
        pl.BlockSpec(memory_space=space) for space in (pltpu.VMEM, pltpu.SMEM, pl.ANY)
    )
    lists = ray_lists * 4 + counts
    dma = pltpu.SemaphoreType.DMA
    return pl.pallas_call(
        kernel,
        out_shape=jax.ShapeDtypeStruct(volume.shape, F32),
        in_specs=[anywhere, anywhere, vmem, smem],
        out_specs=anywhere,
        scratch_shapes=[
            pltpu.VMEM((2, NZ, 8, CY), F32),
            pltpu.VMEM((2, 3, NC, NZ, CH), F32),
            pltpu.VMEM((2, 2, 2, 2 * NA, DR, UC), F32),
            pltpu.VMEM((4, 2, 3, NZ, ROWS), F32),
            pltpu.VMEM((2, 2, NZ, ROWS), F32),
            pltpu.VMEM((4, 2, 8, 128), F32),
            pltpu.VMEM((2, 3 * NZ, 9 * NZ), BF),
            pltpu.VMEM((2, 3 * NZ, 6 * ROWS), BF),
            pltpu.VMEM((2, 3, NC, NZ, CH), F32),
            pltpu.VMEM((2, 3, NC, NZ, CH), F32),
            pltpu.VMEM((2, 2, NC, NZ, CH), F32),
            pltpu.VMEM((2, 2, NC, NZ, CH), F32),
            pltpu.VMEM((2, NC, NZ, CH), F32),
            pltpu.VMEM((2, NC - 1, NZ, CH), F32),
            pltpu.VMEM((2, NC, NZ, CH), F32),
            pltpu.VMEM((NC, NZ, CH), F32),
            pltpu.VMEM((2, 2, NZ, CY), F32),
            pltpu.VMEM((TX // UX, UNC, NZ, CH), F32),
            pltpu.VMEM((2, NZ, CY), F32),
            pltpu.VMEM((NZ, TX, CY), F32),
            dma((10 + TX // 8,)),
            dma((2, 2)), dma((2, 2)),
            dma((3, 2)), dma((3, 2)),
            dma((3,)), dma((3,)),
            dma((2, 2, 2)), dma((2, 2, 2)),
            dma((2, 2, NC)), dma((2, 2, NC)),
            dma((2, 2, NC)), dma((2, 2, NC)),
            dma((2, 2, NC)), dma((2, 2, NC)),
            dma((2, NC)), dma((2, NC)),
            dma((2, NC)), dma((2, NC)), dma((2, NC)),
            dma((2, 2)), dma((2, 2)),
            dma((3, NC)), dma((3, NC)),
            dma((2,)), dma((2,)),
        ],
        compiler_params=pltpu.CompilerParams(
            collective_id=0, has_side_effects=True, vmem_limit_bytes=50 * 1024 * 1024
        ),
        name="sart_tv",
    )(volume, measured, blocks, lists)


def solution(mesh):
    return jax.shard_map(
        per_device,
        mesh=mesh,
        in_specs=(
            P(None, "tile", None),
            P(None, "angle", "tile", None),
            P(None, "angle", "tile", None, None),
            P(None, "angle", "tile"),
            P(None, "angle", "tile"),
        ),
        out_specs=P(None, "tile", None),
        check_vma=False,
    )
```
